32 devices in a mesh: dp: 8 (over y, x, core), seq: 4 (over z).
Axes of the slice: x: 2, y: 2, z: 4, core: 2. Of those that a mesh axis runs over, the one named last changes fastest.
Arguments:
- inputs: bfloat16 [2, 8, 1024, 2048], P(None, 'dp', 'seq'), may hold values from -6 to 6
- cotangent: bfloat16 [2, 8, 1024, 2048], P(None, 'dp', 'seq'), may hold values from -6 to 6
- doc_ids: int32 [2, 8, 1024], P(None, 'dp', 'seq'), may hold values from 0 to 4, as said below
- valid_mask: int32 [2, 8, 1024], P(None, 'dp', 'seq'), may hold values 0 or 1
- gain_attn: bfloat16 [2048], P(('dp', 'seq')), may hold values from 0.5 to 1.5
- w_query: bfloat16 [2048, 2048], P(('dp', 'seq')), may hold values from -0.125 to 0.125
- w_key: bfloat16 [2048, 2048], P(('dp', 'seq')), may hold values from -0.125 to 0.125
- w_value: bfloat16 [2048, 2048], P(('dp', 'seq')), may hold values from -0.125 to 0.125
- w_out: bfloat16 [2048, 2048], P(('dp', 'seq')), may hold values from -1 to 1
- gain_mlp: bfloat16 [2048], P(('dp', 'seq')), may hold values from 0.5 to 1.5
- w_gate: bfloat16 [2048, 8192], P(('dp', 'seq')), may hold values from -0.125 to 0.125
- w_up: bfloat16 [2048, 8192], P(('dp', 'seq')), may hold values from -0.125 to 0.125
- w_down: bfloat16 [8192, 2048], P(('dp', 'seq')), may hold values from -0.0625 to 0.0625
Outputs:
- output: bfloat16 [2, 8, 1024, 2048], P(None, 'dp', 'seq')
- grad_input: bfloat16 [2, 8, 1024, 2048], P(None, 'dp', 'seq')
- grad_gain_attn: float32 [2048], P(('dp', 'seq'))
- grad_query: float32 [2048, 2048], P(('dp', 'seq'))
- grad_key: float32 [2048, 2048], P(('dp', 'seq'))
- grad_value: float32 [2048, 2048], P(('dp', 'seq'))
- grad_out: float32 [2048, 2048], P(('dp', 'seq'))
- grad_gain_mlp: float32 [2048], P(('dp', 'seq'))
- grad_gate: float32 [2048, 8192], P(('dp', 'seq'))
- grad_up: float32 [2048, 8192], P(('dp', 'seq'))
- grad_down: float32 [8192, 2048], P(('dp', 'seq'))
The draws below stay inside these ranges and needn't reach their ends.
Inputs may be any that keep to these rules, and one draw needn't show every extreme that they name: `doc_ids`: document ids along a row start at 0 and never fall; tokens with one id form one document; every row reaches id 4.
All inputs are finite; a program needn't handle non-finite values. No bound on the sum of `valid_mask` on one device may be relied on, other than what follows from the above.
Results may differ from the reference program's by a relative error of at most 0.015.
Values may be sent and summed in bfloat16 or wider, within the bound.
No kernel may reach another device: no remote copies, remote signals or barrier semaphores. Data moves between devices by JAX's collectives and lax.ppermute only.
A program may use at most 768 MiB of HBM per device.

```python
import jax
import jax.numpy as jnp
from jax import lax

D = 2048
FF = 8192
HEADS = 32
HD = 64
SEQ_LEN = 1024
MICRO = 2
ROWS = 8
TOK_DEV = 256


def draw_doc_ids(key, part):
    key = jax.random.fold_in(key, 11)
    key_start, key_end, key_flags = jax.random.split(key, 3)
    grid_shape = (MICRO, ROWS, SEQ_LEN)
    head_room = max(TOK_DEV // 2, 1)
    start_at = jax.random.randint(key_start, (MICRO, ROWS, 1), 2, head_room + 2)
    end_at = jax.random.randint(key_end, (MICRO, ROWS, 1), SEQ_LEN - head_room - 1, SEQ_LEN - 2)
    position = jnp.arange(SEQ_LEN, dtype=jnp.int32)[None, None, :]
    random_starts = (jax.random.randint(key_flags, grid_shape, 0, 8) == 0).astype(jnp.int32)
    new_doc = jnp.where((position > start_at) & (position <= end_at), 0, random_starts)
    new_doc = jnp.where((position == start_at) | (position == end_at + 1), 1, new_doc)
    new_doc = jnp.where((position == 1) | (position == SEQ_LEN - 1), 1, new_doc)
    new_doc = jnp.where(position == 0, 0, new_doc)
    return jnp.minimum(jnp.cumsum(new_doc, axis=-1), 4).astype(jnp.int32)


def plant(array, rng, low, high):
    place = [jax.random.randint(jax.random.fold_in(rng, axis), (), 0, length) for axis, length in enumerate(array.shape)]
    widest = array.shape.index(max(array.shape))
    beside = place[:widest] + [(place[widest] + 1) % array.shape[widest]] + place[widest + 1:]
    return array.at[tuple(place)].set(low).at[tuple(beside)].set(high)


def level_of(rng, extent, cuts, low, high):
    def one(dim, shards_of):
        draws = jax.random.uniform(jax.random.fold_in(jax.random.fold_in(rng, 6), dim), (shards_of,), jnp.float32, low / len(cuts), high / len(cuts))
        return jnp.repeat(jnp.exp(draws), extent[dim] // shards_of).reshape((-1,) + (1,) * (len(extent) - dim - 1))

    factor_of = one(*cuts[0])
    for cut in cuts[1:]:
        factor_of = factor_of * one(*cut)
    return factor_of


def centred(stream_key, shape, spread, bound, cuts=(), kind=jnp.bfloat16):
    values = jax.random.normal(stream_key, shape, jnp.float32) * spread
    if len(cuts) > 0:
        values = level_of(stream_key, shape, cuts, -0.22, 0.18) * values
    return jnp.clip(values, min=-bound, max=bound).astype(kind)


def setup_inputs(seed: int = 0) -> dict:
    streams_of = jax.random.split(jax.random.key(seed), 14)
    return {
        "inputs": centred(streams_of[0], (MICRO, ROWS, SEQ_LEN, D), 1.0, 6.0, ((1, 8), (2, 4))),
        "cotangent": centred(streams_of[1], (MICRO, ROWS, SEQ_LEN, D), 1.0, 6.0, ((1, 8), (2, 4))),
        "doc_ids": draw_doc_ids(jax.random.fold_in(streams_of[13], 71), 0),
        "valid_mask": plant((jax.random.randint(streams_of[3], (MICRO, ROWS, SEQ_LEN), 0, 16) < 15).astype(jnp.int32), jax.random.fold_in(streams_of[3], 1), 0, 1),
        "gain_attn": jnp.clip(1.0 + 0.1 * jax.random.normal(streams_of[4], (D,), jnp.float32), 0.5, 1.5).astype(jnp.bfloat16),
        "w_query": centred(streams_of[5], (D, D), D ** -0.5, 0.125, ((0, 32),)),
        "w_key": centred(streams_of[6], (D, D), D ** -0.5, 0.125, ((0, 32),)),
        "w_value": centred(streams_of[7], (D, D), D ** -0.5, 0.125, ((0, 32),)),
        "w_out": centred(streams_of[8], (D, D), (D // 64) ** -0.5, 1.0, ((0, 32),)),
        "gain_mlp": jnp.clip(1.0 + 0.1 * jax.random.normal(streams_of[9], (D,), jnp.float32), 0.5, 1.5).astype(jnp.bfloat16),
        "w_gate": centred(streams_of[10], (D, FF), D ** -0.5, 0.125, ((0, 32),)),
        "w_up": centred(streams_of[11], (D, FF), D ** -0.5, 0.125, ((0, 32),)),
        "w_down": centred(streams_of[12], (FF, D), FF ** -0.5, 0.0625, ((0, 32),)),
    }


NORM_EPS = 1e-05
ROPE_BASE = 130000.0
MASK_FILL = -1e+30
EXACT = lax.Precision.HIGHEST

@jax.custom_vjp
def low(v):
    return lax.optimization_barrier(v.astype(jnp.bfloat16)).astype(jnp.float32)

@jax.custom_vjp
def low_back(v):
    return v

def low_keep(v):
    return (low(v), None)

def low_pass(kept, grad):
    return (grad,)

def back_keep(v):
    return (v, None)

def back_low(kept, grad):
    return (low(grad),)
low.defvjp(low_keep, low_pass)
low_back.defvjp(back_keep, back_low)

def matmul(left, right):
    return jnp.dot(left, right, precision=EXACT, preferred_element_type=jnp.float32)

def norm_scale(values):
    return lax.rsqrt(lax.optimization_barrier(jnp.mean(values * values, axis=-1, keepdims=True)) + NORM_EPS)

def positions_of(doc_row):
    token_index = jnp.arange(doc_row.shape[0], dtype=jnp.int32)
    before = lax.optimization_barrier(jnp.sum((doc_row[None, :] < doc_row[:, None]).astype(jnp.int32), axis=1)).astype(jnp.int32)
    return token_index - before

def rope_tables(positions, head_dim):
    exponent = jnp.arange(head_dim // 2, dtype=jnp.float32) * (2.0 / head_dim)
    inverse = jnp.power(ROPE_BASE, -exponent)
    angles = positions.astype(jnp.float32)[:, None] * inverse[None, :]
    return (jnp.cos(angles)[:, None, :], jnp.sin(angles)[:, None, :])

def rotate(field_in, cosine_table, sine_table):
    half_width = field_in.shape[-1] // 2
    front_half = field_in[..., :half_width]
    back_half = field_in[..., half_width:]
    return jnp.concatenate([front_half * cosine_table - back_half * sine_table, back_half * cosine_table + front_half * sine_table], axis=-1)

def layer_forward(hidden_in, weight_set, doc_row, valid_row):
    gain_attn, w_query, w_key, w_value, w_out, gain_mlp, w_gate, w_up, w_down = weight_set
    length = hidden_in.shape[0]
    score_scale = float(HD) ** (-0.5)
    normed = low(hidden_in * norm_scale(hidden_in) * gain_attn)
    cosine_table, sine_table = rope_tables(positions_of(doc_row), HD)
    query_raw = low_back(matmul(normed, w_query)).reshape(length, HEADS, HD)
    key_raw = low_back(matmul(normed, w_key)).reshape(length, HEADS, HD)
    values_all = low(low_back(matmul(normed, w_value))).reshape(length, HEADS, HD)
    queries = low(rotate(query_raw, cosine_table, sine_table))
    keys_all = low(rotate(key_raw, cosine_table, sine_table))
    key_pos = jnp.arange(length, dtype=jnp.int32)
    block_rows = min(512, length)

    def attend(row_start):
        query_rows = lax.dynamic_slice_in_dim(queries, row_start, block_rows, 0)
        doc_rows = lax.dynamic_slice_in_dim(doc_row, row_start, block_rows, 0)
        query_pos = row_start + jnp.arange(block_rows, dtype=jnp.int32)
        allowed = (doc_row[None, :] == doc_rows[:, None]) & (key_pos[None, :] <= query_pos[:, None])
        allowed = allowed & ((valid_row[None, :] == 1) | (key_pos[None, :] == query_pos[:, None]))
        scores = low_back(jnp.einsum('thd,jhd->htj', query_rows, keys_all, precision=EXACT) * score_scale)
        masked = jnp.where(allowed[None], scores, MASK_FILL)
        row_top = lax.optimization_barrier(jnp.max(masked, axis=-1, keepdims=True))
        exp_scores = jnp.where(allowed[None], jnp.exp(masked - row_top), 0.0)
        attn_probs = exp_scores / lax.optimization_barrier(jnp.sum(exp_scores, axis=-1, keepdims=True))
        return jnp.einsum('htj,jhd->thd', low(attn_probs), values_all, precision=EXACT)
    starts = (jnp.arange(length // block_rows, dtype=jnp.int32) * block_rows).astype(jnp.int32)
    mixed_heads = lax.map(jax.checkpoint(attend), starts).reshape(length, HEADS * HD)
    attended = low(low_back(mixed_heads))
    middle = hidden_in + low_back(matmul(attended, w_out))
    normed_mlp = low(middle * norm_scale(middle) * gain_mlp)
    gate_proj = low_back(matmul(normed_mlp, w_gate))
    up_proj = low_back(matmul(normed_mlp, w_up))
    activated = low(jax.nn.silu(gate_proj) * up_proj)
    return middle + low_back(matmul(activated, w_down))

def reference(inputs, cotangent, doc_ids, valid_mask, gain_attn, w_query, w_key, w_value, w_out, gain_mlp, w_gate, w_up, w_down):
    params = tuple((weight.astype(jnp.float32) for weight in (gain_attn, w_query, w_key, w_value, w_out, gain_mlp, w_gate, w_up, w_down)))
    micro_count = inputs.shape[0]
    row_count = inputs.shape[1]
    length = inputs.shape[2]
    model_width = inputs.shape[3]
    seq_count = micro_count * row_count
    flat_in = inputs.reshape(seq_count, length, model_width)
    flat_cot = cotangent.reshape(seq_count, length, model_width)
    flat_doc = doc_ids.reshape(seq_count, length)
    flat_valid = valid_mask.reshape(seq_count, length)

    def one_sequence(totals, seq_items):
        seq_in, seq_cot, seq_doc, seq_valid = seq_items

        def forward(hidden_in, *weight_set):
            return layer_forward(hidden_in, weight_set, seq_doc, seq_valid)
        result, pullback = jax.vjp(forward, seq_in.astype(jnp.float32), *params)
        grad_parts = pullback(seq_cot.astype(jnp.float32))
        summed = tuple((total_grad + grad_piece for total_grad, grad_piece in zip(totals, grad_parts[1:])))
        return (summed, (result.astype(jnp.bfloat16), grad_parts[0].astype(jnp.bfloat16)))
    zero_grads = tuple((jnp.zeros_like(param) for param in params))
    totals, (outputs, input_grads) = lax.scan(one_sequence, zero_grads, (flat_in, flat_cot, flat_doc, flat_valid))
    output = outputs.reshape(micro_count, row_count, length, model_width)
    grad_input = input_grads.reshape(micro_count, row_count, length, model_width)
    return (output, grad_input, totals[0], totals[1], totals[2], totals[3], totals[4], totals[5], totals[6], totals[7], totals[8])
```

```python
import functools

import jax
import jax.numpy as jnp
from jax import lax
from jax.experimental import pallas as pl
from jax.experimental.pallas import tpu as pltpu
from jax.sharding import Mesh
from jax.sharding import PartitionSpec as P

HD = 64
NORM_EPS = 1e-05
ROPE_BASE = 130000.0
MASK_FILL = -1e30
LANES = 128
VMEM_BYTES = 56 * 1024 * 1024
F32 = jnp.float32
BF16 = jnp.bfloat16


def dot(left, right):
    return jnp.dot(left, right, preferred_element_type=F32)


def contract_last(left, right):
    return lax.dot_general(left, right, (((1,), (1,)), ((), ())), preferred_element_type=F32)


def contract_first(left, right):
    return lax.dot_general(left, right, (((0,), (0,)), ((), ())), preferred_element_type=F32)


def norm_scale(values):
    return lax.rsqrt(jnp.mean(values * values, axis=-1, keepdims=True) + NORM_EPS)


def norm_back(grad_normed, values, scale_rows, gain):
    unit = values * scale_rows
    scaled = grad_normed * gain
    grad_values = scale_rows * (scaled - unit * jnp.mean(scaled * unit, axis=-1, keepdims=True))
    return (grad_values, jnp.sum(grad_normed * unit, axis=0))


def fill_bias(doc_col, doc_row, bias, block):
    length = bias.shape[0]
    for start in range(0, length, block):
        rows = doc_col[start : start + block, :]
        columns = doc_row[...]
        key_pos = start + lax.broadcasted_iota(jnp.int32, (block, length), 0)
        query_pos = lax.broadcasted_iota(jnp.int32, (block, length), 1)
        same = (rows >> 1) == (columns >> 1)
        open_key = ((rows & 1) == 1) | (key_pos == query_pos)
        allowed = same & (key_pos <= query_pos) & open_key
        bias[start : start + block, :] = jnp.where(allowed, 0.0, MASK_FILL)


def partner(field):
    lane = lax.broadcasted_iota(jnp.int32, field.shape, 1)
    return jnp.where(
        (lane % HD) < HD // 2,
        pltpu.roll(field, LANES - HD // 2, 1),
        pltpu.roll(field, HD // 2, 1),
    )


def split_heads(rows):
    lane = lax.broadcasted_iota(jnp.int32, rows.shape, 1)
    zero = jnp.zeros_like(rows)
    return jnp.concatenate(
        [jnp.where(lane < HD, rows, zero), jnp.where(lane < HD, zero, rows)], axis=0
    )


def join_heads(stacked):
    half = stacked.shape[0] // 2
    lane = lax.broadcasted_iota(jnp.int32, (half, LANES), 1)
    return jnp.where(lane < HD, stacked[:half], stacked[half:])


def attend_kernel(
    block, doc_col, doc_row, cosine, sine, raw, mixed, rotated, log_total, bias
):
    length = bias.shape[0]

    @pl.when(pl.program_id(0) == 0)
    def _():
        fill_bias(doc_col, doc_row, bias, block)

    query = raw[:, 0:LANES]
    key = raw[:, LANES : 2 * LANES]
    scale = float(HD) ** (-0.5)
    query = ((query * cosine[...] + partner(query) * sine[...]) * scale).astype(BF16)
    key = (key * cosine[...] + partner(key) * sine[...]).astype(BF16)
    value = raw[:, 2 * LANES : 3 * LANES].astype(BF16)
    rotated[:, 0:LANES] = query
    rotated[:, LANES : 2 * LANES] = key
    rotated[:, 2 * LANES : 3 * LANES] = value
    value_t = value.T
    for start in range(0, length, block):
        stop = start + block
        stacked = split_heads(query[start:stop])
        scores = contract_last(key[:stop], stacked)
        hide = bias[:stop, start:stop]
        scores = scores + jnp.concatenate([hide, hide], axis=1)
        top = jnp.max(scores, axis=0, keepdims=True)
        weights = jnp.exp(scores - top)
        total = jnp.sum(weights, axis=0, keepdims=True)
        probs = (weights * (1.0 / total)).astype(BF16)
        out_t = dot(value_t[:, :stop], probs)
        mixed[start:stop, :] = join_heads(out_t.T).astype(BF16)
        log_total[0, :, 2 * start : 2 * stop] = top + jnp.log(total)


def attend_back_kernel(
    block, doc_col, doc_row, cosine, sine, rotated, grad_mixed, log_total, grads, bias, key_sum, value_sum
):
    length = bias.shape[0]

    @pl.when(pl.program_id(0) == 0)
    def _():
        fill_bias(doc_col, doc_row, bias, block)

    scale = float(HD) ** (-0.5)
    key = rotated[:, LANES : 2 * LANES]
    value = rotated[:, 2 * LANES : 3 * LANES]
    key_t = key.T
    for start in range(length - block, -1, -block):
        stop = start + block
        queries = split_heads(rotated[start:stop, 0:LANES])
        outs = split_heads(grad_mixed[start:stop, :])
        scores = contract_last(key[:stop], queries)
        hide = bias[:stop, start:stop]
        scores = scores + jnp.concatenate([hide, hide], axis=1)
        probs = jnp.exp(scores - log_total[0, :, 2 * start : 2 * stop])
        grad_probs = contract_last(value[:stop], outs)
        inner = jnp.sum(grad_probs * probs, axis=0, keepdims=True)
        grad_scores = (probs * (grad_probs - inner)).astype(BF16)
        key_part = dot(grad_scores, queries)
        value_part = dot(probs.astype(BF16), outs)
        if stop == length:
            key_sum[...] = key_part
            value_sum[...] = value_part
        else:
            key_sum[:stop, :] += key_part
            value_sum[:stop, :] += value_part
        grad_query = join_heads(dot(key_t[:, :stop], grad_scores).T) * scale
        turned = grad_query * cosine[start:stop, :] - partner(grad_query) * sine[start:stop, :]
        grads[start:stop, 0:LANES] = turned.astype(BF16)
    grad_key = key_sum[...]
    turned = grad_key * cosine[...] - partner(grad_key) * sine[...]
    grads[:, LANES : 2 * LANES] = turned.astype(BF16)
    grads[:, 2 * LANES : 3 * LANES] = value_sum[...].astype(BF16)


def attention_specs(length):
    whole = lambda shape: pl.BlockSpec(shape, lambda pair: (0, 0))
    columns = lambda width: pl.BlockSpec((length, width), lambda pair: (0, pair))
    totals = pl.BlockSpec((1, 1, 2 * length), lambda pair: (pair, 0, 0))
    shared = [whole((length, 1)), whole((1, length)), whole((length, LANES)), whole((length, LANES))]
    return (shared, columns, totals)


def attend(doc_row, cosine, sine, raw):
    length = raw.shape[0]
    pairs = raw.shape[1] // (3 * LANES)
    block = min(256, length)
    shared, columns, totals = attention_specs(length)
    work = pairs * 2 * length * (length + block) * LANES
    return pl.pallas_call(
        functools.partial(attend_kernel, block),
        grid=(pairs,),
        in_specs=shared + [columns(3 * LANES)],
        out_specs=[columns(LANES), columns(3 * LANES), totals],
        out_shape=[
            jax.ShapeDtypeStruct((length, pairs * LANES), BF16),
            jax.ShapeDtypeStruct((length, pairs * 3 * LANES), BF16),
            jax.ShapeDtypeStruct((pairs, 1, 2 * length), F32),
        ],
        scratch_shapes=[pltpu.VMEM((length, length), F32)],
        compiler_params=pltpu.CompilerParams(vmem_limit_bytes=VMEM_BYTES),
        cost_estimate=pl.CostEstimate(
            flops=4 * work, bytes_accessed=20 * length * pairs * LANES, transcendentals=work // LANES
        ),
        name="attend",
    )(doc_row[:, None], doc_row[None, :], cosine, sine, raw)


def attend_back(doc_row, cosine, sine, rotated, grad_mixed, log_total):
    length = rotated.shape[0]
    pairs = rotated.shape[1] // (3 * LANES)
    block = min(256, length)
    shared, columns, totals = attention_specs(length)
    work = pairs * 2 * length * (length + block) * LANES
    return pl.pallas_call(
        functools.partial(attend_back_kernel, block),
        grid=(pairs,),
        in_specs=shared + [columns(3 * LANES), columns(LANES), totals],
        out_specs=columns(3 * LANES),
        out_shape=jax.ShapeDtypeStruct((length, pairs * 3 * LANES), BF16),
        scratch_shapes=[
            pltpu.VMEM((length, length), F32),
            pltpu.VMEM((length, LANES), F32),
            pltpu.VMEM((length, LANES), F32),
        ],
        compiler_params=pltpu.CompilerParams(vmem_limit_bytes=VMEM_BYTES),
        cost_estimate=pl.CostEstimate(
            flops=10 * work, bytes_accessed=14 * length * pairs * LANES, transcendentals=work // LANES
        ),
        name="attend_back",
    )(doc_row[:, None], doc_row[None, :], cosine, sine, rotated, grad_mixed, log_total)


class Axis:
    def __init__(self, name, count):
        self.name = name
        self.count = count

    @property
    def place(self):
        return lax.axis_index(self.name)

    def swap(self, block):
        return lax.ppermute(block, self.name, [(0, 1), (1, 0)])

    def in_order(self, own, other):
        first = self.place == 0
        return jnp.stack([jnp.where(first, own, other), jnp.where(first, other, own)])

    def own(self, blocks):
        return lax.dynamic_index_in_dim(blocks, self.place, 0, keepdims=False)

    def other(self, blocks):
        return lax.dynamic_index_in_dim(blocks, 1 - self.place, 0, keepdims=False)

    def gather(self, block):
        if self.count == 1:
            return block[None]
        if self.count == 2:
            return self.in_order(block, self.swap(block))
        return lax.all_gather(block, self.name, axis=0, tiled=False)

    def exchange(self, blocks):
        if self.count == 1:
            return blocks
        if self.count == 2:
            return self.in_order(self.own(blocks), self.swap(self.other(blocks)))
        return lax.all_to_all(blocks, self.name, split_axis=0, concat_axis=0, tiled=True)

    def scatter(self, blocks):
        if self.count == 1:
            return blocks[0].astype(F32)
        if self.count == 2:
            received = self.swap(self.other(blocks).astype(BF16))
            return self.own(blocks).astype(F32) + received.astype(F32)
        return lax.psum_scatter(
            blocks.astype(BF16), self.name, scatter_dimension=0, tiled=False
        ).astype(F32)


class Line(Axis):
    def exchange(self, blocks):
        count, place = self.count, self.place
        pieces = [lax.dynamic_index_in_dim(blocks, place, 0, keepdims=False)]
        for shift in range(1, count):
            piece = lax.dynamic_index_in_dim(blocks, (place + shift) % count, 0, keepdims=False)
            pairs = [(i, (i + shift) % count) for i in range(count)]
            pieces.append(lax.ppermute(piece, self.name, pairs))
        turned = [pieces[-j % count] for j in range(count)]
        doubled = jnp.stack(turned + turned)
        return lax.dynamic_slice_in_dim(doubled, count - place, count, 0)

    def gather_rows(self, block, axis):
        return lax.all_gather(block, self.name, axis=axis, tiled=True)

    def scatter_rows(self, block, axis):
        return lax.psum_scatter(block, self.name, scatter_dimension=axis, tiled=True)


def on_device(
    sizes,
    inputs,
    cotangent,
    doc_ids,
    valid_mask,
    gain_attn,
    w_query,
    w_key,
    w_value,
    w_out,
    gain_mlp,
    w_gate,
    w_up,
    w_down,
):
    y_axis, x_axis, c_axis, z_axis, t_axis, line = sizes
    micro_count, _, tokens, width = inputs.shape
    rows = w_query.shape[0]
    hidden_units = w_gate.shape[1]
    planes = y_axis.count * x_axis.count
    cores, turns, depth = c_axis.count, t_axis.count, line.count
    part = tokens // (cores * turns)
    own_tokens = depth * part
    length = depth * tokens
    head_block = width // (planes * cores)
    pair_count = head_block // LANES
    hidden_block = hidden_units // (planes * cores)
    everyone = (y_axis.name, x_axis.name, c_axis.name) + line.name

    def to_sequences(block):
        pieces = block[:, 0].reshape(micro_count, cores, turns, part, width)
        pieces = c_axis.exchange(pieces.transpose(1, 0, 2, 3, 4))
        pieces = pieces.transpose(1, 0, 2, 3, 4).reshape(depth, part, width)
        return line.exchange(pieces).reshape(own_tokens, width)

    def from_sequences(block):
        pieces = line.exchange(block.reshape(depth, part, width))
        pieces = pieces.reshape(micro_count, cores, turns, part, width).transpose(1, 0, 2, 3, 4)
        pieces = c_axis.exchange(pieces).transpose(1, 0, 2, 3, 4)
        return pieces.reshape(micro_count, 1, tokens, width)

    def whole_sequence(block):
        pieces = c_axis.gather(t_axis.gather(block.reshape(depth, part, width)))
        return pieces.transpose(2, 0, 1, 3, 4).reshape(length, width)

    def own_share(total):
        pieces = total.reshape(depth, cores, turns, part, width).transpose(1, 2, 0, 3, 4)
        return t_axis.scatter(c_axis.scatter(pieces)).reshape(own_tokens, width)

    def to_group(block):
        return c_axis.gather(x_axis.gather(block)).reshape(-1, width)

    def from_group(total):
        pieces = total.reshape(cores, x_axis.count, own_tokens, width)
        return x_axis.scatter(c_axis.scatter(pieces))

    packed = lax.all_gather(
        doc_ids[:, 0] * 2 + valid_mask[:, 0], (c_axis.name,) + line.name, axis=0, tiled=False
    ).reshape(cores, depth, micro_count, tokens)
    gains = lax.all_gather(
        jnp.concatenate([gain_attn, gain_mlp])[None], everyone, axis=0, tiled=True
    )
    gains = gains.reshape(-1, 2, rows).transpose(1, 0, 2).reshape(2, width).astype(F32)

    own_in = to_sequences(inputs)

    joined = jnp.stack([w_query, w_key, w_value], axis=1)
    joined = joined.reshape(rows, 3, planes, cores, pair_count, LANES)
    joined = joined.transpose(3, 0, 2, 4, 1, 5).reshape(cores, rows, 3 * width // cores)
    joined = line.gather_rows(c_axis.exchange(joined), 1)
    w_qkv = x_axis.gather(y_axis.gather(joined)).transpose(1, 0, 2, 3, 4).reshape(width, -1)
    own_out = line.gather_rows(w_out, 0)
    own_out = x_axis.gather(y_axis.gather(own_out)).transpose(1, 0, 2, 3).reshape(-1, width)

    def hidden_columns(weight):
        pieces = weight.reshape(rows, y_axis.count, x_axis.count, cores, hidden_block)
        pieces = pieces.transpose(3, 2, 0, 1, 4).reshape(cores, x_axis.count, rows, -1)
        pieces = x_axis.exchange(c_axis.exchange(pieces).transpose(1, 0, 2, 3))
        pieces = line.gather_rows(pieces.reshape(x_axis.count * cores, rows, -1), 1)
        return y_axis.gather(pieces).reshape(width, -1)

    own_gate = hidden_columns(w_gate)
    own_up = hidden_columns(w_up)
    own_down = y_axis.gather(line.gather_rows(w_down, 0)).reshape(-1, width)
    own_cotangent = to_sequences(cotangent)
    group_cotangent = to_group(own_cotangent)

    share = planes // turns
    if turns > 1:
        turn = t_axis.place * share
        qkv_blocks = w_qkv.reshape(width, planes, -1)
        w_qkv = lax.dynamic_slice_in_dim(qkv_blocks, turn, share, 1).reshape(width, -1)
        out_blocks = own_out.reshape(planes, -1, width)
        own_out = lax.dynamic_slice_in_dim(out_blocks, turn, share, 0).reshape(-1, width)

    z_place = lax.axis_index(z_axis.name)
    doc_row = lax.dynamic_index_in_dim(packed, z_place % cores, 0, keepdims=False)
    doc_row = lax.dynamic_index_in_dim(doc_row, z_place // cores, 1, keepdims=False).reshape(length)
    document = doc_row >> 1
    before = jnp.sum((document[None, :] < document[:, None]).astype(jnp.int32), axis=1)
    positions = (jnp.arange(length, dtype=jnp.int32) - before).astype(F32)
    lane = jnp.arange(LANES, dtype=jnp.int32)
    exponent = (lane % (HD // 2)).astype(F32) * (2.0 / HD)
    angles = positions[:, None] * jnp.power(ROPE_BASE, -exponent)[None, :]
    cosine = jnp.cos(angles)
    sine = jnp.where((lane % HD) < HD // 2, -1.0, 1.0)[None, :] * jnp.sin(angles)

    all_in = whole_sequence(own_in).astype(F32)
    normed = (all_in * norm_scale(all_in) * gains[0]).astype(BF16)
    mixed, rotated, log_total = attend(doc_row, cosine, sine, dot(normed, w_qkv))
    hidden_in = own_in.astype(F32)
    middle = hidden_in + own_share(dot(mixed, own_out))

    scale_mid = norm_scale(middle)
    normed_mlp = to_group((middle * scale_mid * gains[1]).astype(BF16))
    gate_proj = dot(normed_mlp, own_gate)
    up_proj = dot(normed_mlp, own_up)
    sigmoid_gate = jax.nn.sigmoid(gate_proj)
    silu_gate = gate_proj * sigmoid_gate
    activated = (silu_gate * up_proj).astype(BF16)
    result = middle + from_group(dot(activated, own_down))
    output = from_sequences(result.astype(BF16))

    grad_activated = contract_last(group_cotangent, own_down)
    grad_gate = (
        grad_activated * up_proj * sigmoid_gate * (1.0 + gate_proj * (1.0 - sigmoid_gate))
    ).astype(BF16)
    grad_up = (grad_activated * silu_gate).astype(BF16)
    grad_normed_mlp = from_group(contract_last(grad_gate, own_gate) + contract_last(grad_up, own_up))
    grad_mid_norm, gain_mlp_term = norm_back(grad_normed_mlp, middle, scale_mid, gains[1])
    grad_middle = own_cotangent.astype(F32) + grad_mid_norm

    def scatter_hidden_rows(grad):
        half = y_axis.scatter(grad.astype(BF16).reshape(y_axis.count, -1, width))
        return line.scatter_rows(half.astype(BF16), 0)

    def scatter_hidden_columns(grad):
        half = y_axis.scatter(
            grad.astype(BF16).reshape(y_axis.count, x_axis.count * cores, depth, rows, -1)
        )
        half = half.astype(BF16).transpose(1, 0, 2, 3).reshape(depth * x_axis.count * cores * rows, -1)
        mine = line.scatter_rows(half, 0).reshape(x_axis.count, cores, rows, -1)
        mine = x_axis.exchange(mine).transpose(1, 0, 2, 3)
        mine = c_axis.exchange(mine).reshape(cores, x_axis.count, rows, y_axis.count, hidden_block)
        return mine.transpose(2, 3, 1, 0, 4).reshape(rows, hidden_units).astype(F32)

    grad_gate_shard = scatter_hidden_columns(contract_first(normed_mlp, grad_gate))
    grad_up_shard = scatter_hidden_columns(contract_first(normed_mlp, grad_up))
    grad_down_shard = scatter_hidden_rows(contract_first(activated, group_cotangent)).astype(F32)

    grad_branch = whole_sequence(grad_middle.astype(BF16))
    grad_mixed = contract_last(grad_branch, own_out).astype(BF16)
    grad_out = contract_first(mixed, grad_branch).astype(BF16)
    grad_raw = attend_back(doc_row, cosine, sine, rotated, grad_mixed, log_total)
    grad_normed = own_share(contract_last(grad_raw, w_qkv))
    grad_in_norm, gain_attn_term = norm_back(
        grad_normed, hidden_in, norm_scale(hidden_in), gains[0]
    )
    grad_input = from_sequences((grad_middle + grad_in_norm).astype(BF16))
    grad_qkv = contract_first(normed, grad_raw).astype(BF16)
    if turns > 1:
        blocks = grad_qkv.reshape(width, share, -1)
        blank = jnp.zeros((width, planes, blocks.shape[2]), BF16)
        grad_qkv = lax.dynamic_update_slice_in_dim(blank, blocks, turn, 1).reshape(width, -1)
        blocks = grad_out.reshape(share, -1, width)
        blank = jnp.zeros((planes, blocks.shape[1], width), BF16)
        grad_out = lax.dynamic_update_slice_in_dim(blank, blocks, turn, 0).reshape(-1, width)

    def scatter_planes(grad, trailing):
        pieces = grad.reshape((y_axis.count, x_axis.count) + trailing)
        pieces = x_axis.scatter(pieces.transpose((1, 0) + tuple(range(2, pieces.ndim))))
        return y_axis.scatter(pieces.astype(BF16)).astype(BF16)

    grad_out_shard = line.scatter_rows(scatter_planes(grad_out, (depth * rows, width)), 0)
    mine = scatter_planes(grad_qkv, (cores, depth, rows, 3 * width // cores))
    mine = mine.transpose(1, 0, 2, 3).reshape(depth * cores * rows, -1)
    mine = c_axis.exchange(line.scatter_rows(mine, 0).reshape(cores, rows, -1))
    mine = mine.reshape(cores, rows, planes, pair_count, 3, LANES).transpose(4, 1, 2, 0, 3, 5)
    mine = mine.reshape(3, rows, width).astype(F32)

    terms = jnp.stack([gain_attn_term, gain_mlp_term])
    for axis in (c_axis, x_axis, y_axis, z_axis, t_axis):
        if axis.count == 1:
            continue
        if axis.count == 2:
            terms = terms + axis.swap(terms)
        else:
            terms = lax.psum(terms, axis.name)
    rank = lax.axis_index(everyone)
    terms = lax.dynamic_slice_in_dim(terms, rank * rows, rows, 1)

    return (
        output,
        grad_input,
        terms[0],
        mine[0],
        mine[1],
        mine[2],
        grad_out_shard.astype(F32),
        terms[1],
        grad_gate_shard,
        grad_up_shard,
        grad_down_shard,
    )


def solution(mesh):
    dp, seq = mesh.shape["dp"], mesh.shape["seq"]
    names = ("y", "x", "c", "z", "t")

    def step(*arrays):
        micro_count = arrays[0].shape[0]
        turns = seq // (2 * micro_count)
        shape = (2, dp // 4, 2, seq // turns, turns)
        fine = Mesh(mesh.devices.reshape(shape), names)
        axes = [Axis(name, count) for name, count in zip(names, shape)]
        sizes = tuple(axes) + (Line(("z", "t"), seq),)
        row, shard = ("y", "x", "c"), ("y", "x", "c", "z", "t")
        tokens_at = P(None, row, ("z", "t"), None)
        ids_at = P(None, row, ("z", "t"))
        vector, matrix = P(shard), P(shard, None)
        return jax.shard_map(
            functools.partial(on_device, sizes),
            mesh=fine,
            in_specs=(tokens_at, tokens_at, ids_at, ids_at, vector)
            + (matrix,) * 4
            + (vector,)
            + (matrix,) * 3,
            out_specs=(tokens_at, tokens_at, vector)
            + (matrix,) * 4
            + (vector,)
            + (matrix,) * 3,
            check_vma=False,
        )(*arrays)

    return step
```
